128 devices in a mesh: row: 8 (over y, z_hi), col: 16 (over x, z_lo, core).
Axes of the slice: x: 4, y: 4, z: 4 (z_hi: 2, z_lo: 2; z = z_hi * 2 + z_lo), core: 2. Of those that a mesh axis runs over, the one named last changes fastest.
Arguments:
- panel_left: bfloat16 [5000, 128, 128], P(None, ('row', 'col')), may hold values from -0.078125 to 0.078125
- panel_right: bfloat16 [5000, 128, 128], P(None, ('row', 'col')), may hold values from -6 to 6
- amplitudes: bfloat16 [256, 128, 128], P('col', 'row'), may hold values from -0.046875 to 0.046875
- eps_virtual: float32 [1600], replicated, may hold values from 0.2 to 1.5
- eps_occupied: float32 [100], replicated, may hold values from -1.5 to -0.3
- pair_list: int32 [256, 2], replicated, may hold values from 0 to 99
- blocks: int32 [2], replicated, may hold values from 0 to 11
Outputs:
- update: bfloat16 [256, 128, 128], P('col', 'row')
The draws below stay inside these ranges and needn't reach their ends.
All inputs are finite; a program needn't handle non-finite values.
Results may differ from the reference program's by a relative error of at most 0.0049.
Values may be sent and summed in bfloat16 or wider, within the bound.
No kernel may reach another device: no remote copies, remote signals or barrier semaphores. Data moves between devices by JAX's collectives and lax.ppermute only.
A program may use at most 128 MiB of HBM per device.

```python
import jax
import jax.numpy as jnp
from jax import lax

V = 1600
NQ = 5000
NOCC = 100
CB = 128
PAIRS = 256
VWIN = 128


def place_ends(entries, own_key, least, top_value):
    longest = entries.shape.index(max(entries.shape))
    spots = []
    for shift in (0, 1):
        where = [jax.random.randint(jax.random.fold_in(own_key, axis), (), 0, length) for axis, length in enumerate(entries.shape)]
        where[longest] = (where[longest] + shift) % entries.shape[longest]
        spots.append(tuple(where))
    return entries.at[spots[0]].set(least).at[spots[1]].set(top_value)


def shard_levels(key, dims, split, least, high):
    level, own = 1.0, jax.random.fold_in(key, 6)
    for axis_at, shards_of in split:
        draws = jnp.exp(jax.random.uniform(jax.random.fold_in(own, axis_at), (shards_of,), jnp.float32, least / len(split), high / len(split)))
        level = level * jnp.repeat(draws, dims[axis_at] // shards_of).reshape([-1 if axis == axis_at else 1 for axis in range(len(dims))])
    return level


def noise(rng, shape, spread, bound, shards=(), held_as=jnp.bfloat16):
    loudness = shard_levels(rng, shape, shards, -0.22, 0.18) if shards else 1.0
    entries = jax.random.normal(rng, shape, jnp.float32) * spread * loudness
    return jnp.minimum(jnp.maximum(entries, -bound), bound).astype(held_as)


def setup_inputs(seed: int = 0) -> dict:
    keys = jax.random.split(jax.random.key(seed), 8)
    return {
        "panel_left": noise(keys[0], (NQ, VWIN, CB), NQ ** -0.5, 0.078125, ((1, 128),)),
        "panel_right": noise(keys[1], (NQ, VWIN, CB), 1.0, 6.0, ((1, 128),)),
        "amplitudes": noise(keys[2], (PAIRS, CB, CB), (CB * CB) ** -0.5, 0.046875, ((0, 16), (1, 8))),
        "eps_virtual": jnp.clip(jax.random.uniform(keys[3], (V,), jnp.float32, 0.2, 1.5), 0.2, 1.5),
        "eps_occupied": jnp.clip(jax.random.uniform(keys[4], (NOCC,), jnp.float32, -1.5, -0.3), -1.5, -0.3),
        "pair_list": place_ends(jax.random.randint(keys[5], (PAIRS, 2), 0, NOCC), jax.random.fold_in(keys[5], 1), 0, NOCC - 1).astype(jnp.int32),
        "blocks": jax.random.randint(keys[6], (2,), 0, V // VWIN).astype(jnp.int32),
    }


def reference(panel_left, panel_right, amplitudes, eps_virtual, eps_occupied, pair_list, blocks):
    right_flat = panel_right.astype(jnp.float32).reshape(NQ, VWIN * CB)
    amp_float = amplitudes.astype(jnp.float32)

    def one_row(left_slice):
        block_sum = lax.dot_general(left_slice.astype(jnp.float32), right_flat, (((0,), (0,)), ((), ())), precision=lax.Precision.HIGHEST, preferred_element_type=jnp.float32)
        rounded = lax.optimization_barrier(block_sum.astype(jnp.bfloat16))
        integrals = rounded.astype(jnp.float32).reshape(CB, VWIN, CB)
        return jnp.einsum("cbd,pcd->pb", integrals, amp_float, precision=lax.Precision.HIGHEST)

    ladder = lax.map(one_row, jnp.moveaxis(panel_left, 1, 0))
    ladder = jnp.transpose(ladder, (1, 0, 2))
    first_energy = lax.dynamic_slice_in_dim(eps_virtual, (blocks[0] * VWIN).astype(jnp.int32), VWIN)
    second_energy = lax.dynamic_slice_in_dim(eps_virtual, (blocks[1] * VWIN).astype(jnp.int32), VWIN)
    pair_sum = eps_occupied[pair_list[:, 0]] + eps_occupied[pair_list[:, 1]]
    denominator = first_energy[None, :, None] + second_energy[None, None, :] - pair_sum[:, None, None]
    return (ladder / denominator).astype(jnp.bfloat16)
```

```python
import jax
import jax.numpy as jnp
from jax import lax
from jax.experimental import pallas as pl
from jax.experimental.pallas import tpu as pltpu
from jax.sharding import Mesh, PartitionSpec as P

Z = ("zh", "zl")
ALL = ("y", "zh", "x", "zl", "c")
QP = 1280
W = 128
ROWS = 512
STRIDE = 520
CH = 64


def shift(value, axis, step):
    return lax.ppermute(value, axis, [(i, (i + step) % 4) for i in range(4)])


def ladder_kernel(place, left, r_own, r_m, r_p, r_h0, r_h1, t0, t1, t2, t3, u0, u1, u2, u3, out, lbuf, rbuf, tbuf, scr, acc, sems):
    copies_r = [
        pltpu.make_async_copy(r_own, rbuf.at[pl.ds(0, 4)], sems.at[0]),
        pltpu.make_async_copy(r_m, rbuf.at[pl.ds(4, 4)], sems.at[1]),
        pltpu.make_async_copy(r_p, rbuf.at[pl.ds(8, 4)], sems.at[2]),
        pltpu.make_async_copy(r_h0, rbuf.at[pl.ds(12, 2)], sems.at[3]),
        pltpu.make_async_copy(r_h1, rbuf.at[pl.ds(14, 2)], sems.at[4]),
    ]
    copies_l = [pltpu.make_async_copy(left.at[pl.ds(8 * k, 8)], lbuf.at[pl.ds(8 * k, 8)], sems.at[5 + k]) for k in range(4)]
    copies_t = []
    for k, ref in enumerate((t0, t1, t2, t3)):
        copies_t.append(pltpu.make_async_copy(ref, tbuf.at[place[k], place[4]], sems.at[9 + k]))
    for k, ref in enumerate((u0, u1, u2, u3)):
        copies_t.append(pltpu.make_async_copy(ref, tbuf.at[place[k], place[5]], sems.at[13 + k]))
    copies_l[0].start()
    for copy in copies_r:
        copy.start()
    for copy in copies_l[1:]:
        copy.start()
    for copy in copies_t:
        copy.start()
    for copy in copies_r:
        copy.wait()
    acc[...] = jnp.zeros_like(acc)
    for phase in range(2):
        for part in range(4):
            if phase == 0:
                copies_l[part].wait()
            rows = lbuf[pl.ds(part * 8, 8), pl.ds(phase * CH, CH), :].reshape(8 * CH, QP)

            def integrals(group, carry):
                weights = rbuf[pl.ds(group * 4, 4)].reshape(4 * W, QP)
                m = lax.dot_general(rows, weights, (((1,), (1,)), ((), ())), preferred_element_type=jnp.float32)
                for k in range(8):
                    c_core, zh, zl = k // 4, (k // 2) % 2, k % 2
                    slot = zh * 256 + ((part * 2 + zl) * 2 + c_core) * 16
                    for b in range(4):
                        scr[pl.ds(slot + group * 4 + b, CH, stride=STRIDE), :] = m[k * CH : (k + 1) * CH, b * W : (b + 1) * W]
                return carry

            lax.fori_loop(0, 4, integrals, 0)
        if phase == 0:
            for copy in copies_t:
                copy.wait()

        def contract(step, carry):
            x = []
            t = []
            for k in range(8):
                cc = step * 8 + k
                x.append(scr[pl.ds(pl.multiple_of(cc * STRIDE, 8), ROWS), :].astype(jnp.bfloat16))
                c = phase * CH + cc
                y, zh, low = c // 32, (c // 16) % 2, c % 16
                t.append(
                    jnp.concatenate(
                        [tbuf[zh * 2 + zl, core, y * 4 + xx, low] for xx in range(4) for zl in range(2) for core in range(2)],
                        axis=0,
                    )
                )
            acc[...] += lax.dot_general(
                jnp.concatenate(t, axis=1),
                jnp.concatenate(x, axis=1),
                (((1,), (1,)), ((), ())),
                preferred_element_type=jnp.float32,
            )
            return carry

        lax.fori_loop(0, CH // 8, contract, 0)
    for half in range(2):
        out[half] = acc[:, half * 256 : (half + 1) * 256]


def ladder(place, left, rights, ts):
    anywhere = pl.BlockSpec(memory_space=pl.ANY)
    return pl.pallas_call(
        ladder_kernel,
        out_shape=jax.ShapeDtypeStruct((2, 256, 256), jnp.float32),
        in_specs=[pl.BlockSpec(memory_space=pltpu.SMEM)] + [anywhere] * 14,
        out_specs=pl.BlockSpec(memory_space=pltpu.VMEM),
        scratch_shapes=[
            pltpu.VMEM((32, W, QP), jnp.bfloat16),
            pltpu.VMEM((16, W, QP), jnp.bfloat16),
            pltpu.VMEM((4, 2, 16, 16, 16, W), jnp.bfloat16),
            pltpu.VMEM((CH * STRIDE, W), jnp.float32),
            pltpu.VMEM((256, ROWS), jnp.float32),
            pltpu.SemaphoreType.DMA((17,)),
        ],
        compiler_params=pltpu.CompilerParams(vmem_limit_bytes=58 * 2**20),
        cost_estimate=pl.CostEstimate(flops=26 * 10**9, bytes_accessed=25 * 10**6, transcendentals=0),
    )(place, left, *rights, *ts)


def shards(panel_left, panel_right, amplitudes, eps_virtual, eps_occupied, pair_list, blocks):
    y, zh, x, zl, core = (lax.axis_index(name) for name in ALL)
    z = zh * 2 + zl
    panels = jnp.stack([panel_left[:, 0, :], panel_right[:, 0, :]])
    panels = jnp.pad(panels, ((0, 0), (0, 4 * QP - panels.shape[1]), (0, 0)))
    panels = jnp.transpose(panels.reshape(2, 4, QP, W), (1, 0, 3, 2))
    panels = lax.all_to_all(panels, Z, 0, 0, tiled=True)
    left_part, right_part = panels[:, 0], panels[:, 1]
    left = lax.all_gather(left_part, ("x", "c"), axis=0, tiled=True)
    r_m = shift(right_part, "y", 1)
    r_p = shift(right_part, "y", -1)
    r_h0 = shift(r_m[:2], "y", 1)
    r_h1 = shift(r_p[2:], "y", -1)
    own_t = jnp.transpose(amplitudes, (1, 0, 2))
    t0 = lax.all_to_all(jnp.broadcast_to(own_t[None], (16,) + own_t.shape), ("y", "x"), 0, 0, tiled=True)
    ts = [t0, shift(t0, Z, 1), shift(t0, Z, -1), shift(t0, Z, 2)]
    ts = ts + [lax.ppermute(t, "c", [(0, 1), (1, 0)]) for t in ts]
    place = jnp.stack([z, (z + 3) % 4, (z + 1) % 4, (z + 2) % 4, core, 1 - core]).astype(jnp.int32)
    partial = ladder(place, left, (right_part, r_m, r_p, r_h0, r_h1), ts)
    gathered = lax.all_to_all(partial.reshape(32, 16, 256), ("zh", "x", "zl", "c"), 0, 0, tiled=True)
    summed = jnp.sum(gathered.reshape(2, 4, 2, 2, 16, 256), axis=(0, 2))
    summed = summed.reshape(4, 2, 16, 16, 4, 4)
    order = (jnp.array([0, 1, 3, 2], jnp.int32))
    relative = jnp.take(summed, jnp.array([0, 2, 3, 1]), axis=4)
    doubled = jnp.concatenate([relative, relative], axis=4)
    absolute = lax.dynamic_slice_in_dim(doubled, (4 - y) % 4, 4, axis=4)
    absolute = absolute.reshape(4, 2, 16, 16, 4, 2, 2)
    block = jnp.transpose(absolute, (2, 3, 4, 5, 0, 6, 1)).reshape(16, 16, W)
    first = lax.dynamic_slice_in_dim(eps_virtual, blocks[0] * W + (y * 2 + zh) * 16, 16)
    second = lax.dynamic_slice_in_dim(eps_virtual, blocks[1] * W, W)
    pairs = lax.dynamic_slice_in_dim(pair_list, ((x * 2 + zl) * 2 + core) * 16, 16, axis=0)
    levels = jnp.arange(eps_occupied.shape[0], dtype=jnp.int32)
    picked = jnp.where(pairs[:, :, None] == levels[None, None, :], eps_occupied[None, None, :], 0.0)
    pair_sum = jnp.sum(picked, axis=(1, 2))
    denominator = first[None, :, None] + second[None, None, :] - pair_sum[:, None, None]
    return (block / denominator).astype(jnp.bfloat16)


def solution(mesh):
    fine = Mesh(mesh.devices.reshape(4, 2, 4, 2, 2), ALL)
    return jax.shard_map(
        shards,
        mesh=fine,
        in_specs=(
            P(None, ALL, None),
            P(None, ALL, None),
            P(("x", "zl", "c"), ("y", "zh"), None),
            P(),
            P(),
            P(),
            P(),
        ),
        out_specs=P(("x", "zl", "c"), ("y", "zh"), None),
        check_vma=False,
    )
```

```python
import jax
import jax.numpy as jnp
from jax import lax
from jax.experimental import pallas as pl
from jax.experimental.pallas import tpu as pltpu
from jax.sharding import Mesh, PartitionSpec as P

Z = ("zh", "zl")
ALL = ("y", "zh", "x", "zl", "c")
RING = (0, 3, 1, 2)
QP = 1280
W = 128
NEAR = 96
FAR = 32
ANYWHERE = pl.BlockSpec(memory_space=pl.ANY)
SCALARS = pl.BlockSpec(memory_space=pltpu.SMEM)
LIMIT = 58 * 2**20


def gate(values, after):
    count = len(values)

    def nothing(*refs):
        pass

    return pl.pallas_call(
        nothing,
        out_shape=[jax.ShapeDtypeStruct(v.shape, v.dtype) for v in values],
        in_specs=[ANYWHERE] * (count + len(after)),
        out_specs=[ANYWHERE] * count,
        input_output_aliases={k: k for k in range(count)},
        name="gate",
    )(*values, *after)


def block_integrals(place, left, right, core, scr, base, stride, first):
    m = lax.dot_general(
        left.reshape(4 * W, QP), right.reshape(4 * W, QP), (((1,), (1,)), ((), ())), preferred_element_type=jnp.float32
    )
    for za in range(4):
        for zb in range(4):
            row = base + first + place[za] * 8 + place[zb] * 2 + core
            scr[pl.ds(row, W, stride=stride), :] = m[za * W : (za + 1) * W, zb * W : (zb + 1) * W]


def near_kernel(place, l0, l1, l2, r0, r1, r2, r3, r4, r5, xs, lbuf, rbuf, scr, xbuf, sems):
    copies_l = [pltpu.make_async_copy(ref, lbuf.at[u], sems.at[8 + u]) for u, ref in enumerate((l0, l1, l2))]
    rights = (r0, r1, r2, r3, r4, r5)
    copies_r = [pltpu.make_async_copy(ref, rbuf.at[g], sems.at[g]) for g, ref in enumerate(rights)]
    copies_l[0].start()
    for copy in copies_r:
        copy.start()
    for copy in copies_l[1:]:
        copy.start()
    stride = NEAR + 8
    stores = [pltpu.make_async_copy(xbuf.at[u], xs.at[u], sems.at[11 + u]) for u in range(3)]
    for u in range(3):
        copies_l[u].wait()

        def block(g, carry):
            if u == 0:
                pltpu.make_async_copy(r0, rbuf.at[g], sems.at[g]).wait()
            block_integrals(place, lbuf[u], rbuf[g], place[4 + g], scr, u * W * stride, stride, (g // 2) * 32)
            return carry

        lax.fori_loop(0, 6, block, 0)

        def convert(c, carry):
            start = pl.multiple_of((u * W + c) * stride, 8)
            xbuf[u, c] = scr[pl.ds(start, NEAR), :].astype(jnp.bfloat16)
            return carry

        lax.fori_loop(0, W, convert, 0, unroll=8)
        stores[u].start()
    for copy in stores:
        copy.wait()


def near_integrals(place, lefts, rights):
    return pl.pallas_call(
        near_kernel,
        out_shape=jax.ShapeDtypeStruct((3, W, NEAR, W), jnp.bfloat16),
        in_specs=[SCALARS] + [ANYWHERE] * 9,
        out_specs=ANYWHERE,
        scratch_shapes=[
            pltpu.VMEM((3, 4, W, QP), jnp.bfloat16),
            pltpu.VMEM((6, 4, W, QP), jnp.bfloat16),
            pltpu.VMEM((3 * W * (NEAR + 8), W), jnp.float32),
            pltpu.VMEM((3, W, NEAR, W), jnp.bfloat16),
            pltpu.SemaphoreType.DMA((14,)),
        ],
        compiler_params=pltpu.CompilerParams(vmem_limit_bytes=LIMIT),
        cost_estimate=pl.CostEstimate(flops=15 * 10**9, bytes_accessed=10**7, transcendentals=0),
        name="near_integrals",
    )(place, *lefts, *rights)


def far_kernel(place, xs, l0, l1, l2, l3, amps, *refs):
    rights, (out, lbuf, rbuf, tbuf, xbuf, scr, scr3, acc, sems, t_sem) = refs[:8], refs[8:]
    copies_l = [pltpu.make_async_copy(ref, lbuf.at[u], sems.at[8 + u]) for u, ref in enumerate((l0, l1, l2, l3))]
    copies_r = [pltpu.make_async_copy(ref, rbuf.at[g], sems.at[g]) for g, ref in enumerate(rights)]
    copy_x = pltpu.make_async_copy(xs, xbuf.at[:, :, pl.ds(0, NEAR), :], sems.at[12])
    copies_t = [
        pltpu.make_async_copy(amps.at[:, jy, jx], tbuf.at[:, place[16 + jy] * 4 + place[20 + jx]], t_sem)
        for jy in range(4)
        for jx in range(4)
    ]
    for g in (6, 7):
        copies_r[g].start()
    for copy in copies_l:
        copy.start()
    for copy in copies_r[:6]:
        copy.start()
    copy_x.start()
    for copy in copies_t:
        copy.start()
    for copy in copies_l + copies_r[6:]:
        copy.wait()
    stride = FAR + 8

    def opposite(u, carry):
        for g in (6, 7):
            block_integrals(place, lbuf[u], rbuf[g], place[4 + g], scr, u * W * stride, stride, 0)
        return carry

    lax.fori_loop(0, 3, opposite, 0)
    stride3 = NEAR + FAR + 8

    def last(g, carry):
        @pl.when(g < 6)
        def _():
            pltpu.make_async_copy(l0, rbuf.at[g], sems.at[g]).wait()

        block_integrals(place, lbuf[3], rbuf[g], place[4 + g], scr3, 0, stride3, (g // 2) * 32)
        return carry

    lax.fori_loop(0, 8, last, 0)
    copy_x.wait()
    for copy in copies_t:
        copy.wait()
    acc[...] = jnp.zeros_like(acc)

    def contract(step, carry):
        x = []
        t = []
        for k in range(16):
            c = step * 16 + k
            last = scr3[pl.ds(pl.multiple_of(c * stride3, 8), NEAR + FAR), :].astype(jnp.bfloat16)
            pieces = []
            for u in range(3):
                start = pl.multiple_of((u * W + c) * stride, 8)
                far = scr[pl.ds(start, FAR), :].astype(jnp.bfloat16)
                near = xbuf[u, c, :NEAR]
                pieces.append([near[s * 32 : s * 32 + 32] for s in range(3)] + [far])
            pieces.append([last[s * 32 : s * 32 + 32] for s in range(4)])
            rows = [pieces[u][s][zh * 16 : zh * 16 + 16] for zh in range(2) for u in range(4) for s in range(4)]
            x.append(jnp.concatenate(rows, axis=0))
            y, zh, low = c // 32, (c // 16) % 2, c % 16
            t.append(
                jnp.concatenate(
                    [tbuf[(zh * 2 + zl) * 2 + core, y * 4 + xx, low] for xx in range(4) for zl in range(2) for core in range(2)],
                    axis=0,
                )
            )
        acc[...] += lax.dot_general(
            jnp.concatenate(t, axis=1),
            jnp.concatenate(x, axis=1),
            (((1,), (1,)), ((), ())),
            preferred_element_type=jnp.float32,
        )
        return carry

    lax.fori_loop(0, W // 16, contract, 0)
    for zh in range(2):
        out[zh] = acc[:, zh * 256 : (zh + 1) * 256].astype(out.dtype).reshape(16, 16, 256)


def far_ladder(place, xs, lefts, amps, rights):
    return pl.pallas_call(
        far_kernel,
        out_shape=jax.ShapeDtypeStruct((2, 16, 16, 256), jnp.bfloat16),
        in_specs=[SCALARS] + [ANYWHERE] * 14,
        out_specs=pl.BlockSpec(memory_space=pltpu.VMEM),
        scratch_shapes=[
            pltpu.VMEM((4, 4, W, QP), jnp.bfloat16),
            pltpu.VMEM((8, 4, W, QP), jnp.bfloat16),
            pltpu.VMEM((8, 16, 16, 16, W), jnp.bfloat16),
            pltpu.VMEM((3, W, NEAR, W), jnp.bfloat16),
            pltpu.VMEM((3 * W * (FAR + 8), W), jnp.float32),
            pltpu.VMEM((W * (NEAR + FAR + 8), W), jnp.float32),
            pltpu.VMEM((256, 512), jnp.float32),
            pltpu.SemaphoreType.DMA((13,)),
            pltpu.SemaphoreType.DMA,
        ],
        compiler_params=pltpu.CompilerParams(vmem_limit_bytes=LIMIT),
        cost_estimate=pl.CostEstimate(flops=15 * 10**9, bytes_accessed=10**7, transcendentals=0),
        name="far_ladder",
    )(place, xs, *lefts, amps, *rights)


def swap(value):
    return lax.ppermute(value, "c", [(0, 1), (1, 0)])


def shift(value, axis, step):
    return lax.ppermute(value, axis, [(i, (i + step) % 4) for i in range(4)])


def onward(value, axis):
    pairs = [(i * 2 + c, (i + 1 - 2 * c) % 4 * 2 + c) for i in range(4) for c in range(2)]
    return lax.ppermute(value, (axis, "c"), pairs)


def over_ring(value, axis):
    return jnp.stack([value, shift(value, axis, 1), shift(value, axis, -1), shift(value, axis, 2)])


def place_units():
    table = []
    for x in range(4):
        for other in range(4):
            for c in range(2):
                step = (other - x) % 4
                if step in (0, 2):
                    core, unit = c, (0 if step == 0 else 3)
                else:
                    core = 0 if step == 3 else 1
                    unit = 1 if core == c else 2
                table.append(x * 8 + core * 4 + unit)
    return table


def shards(panel_left, panel_right, amplitudes, eps_virtual, eps_occupied, pair_list, blocks):
    y, zh, x, zl, core = (lax.axis_index(name) for name in ALL)
    z = zh * 2 + zl
    panels = jnp.stack([panel_left[:, 0, :], panel_right[:, 0, :]])
    panels = jnp.pad(panels, ((0, 0), (0, 4 * QP - panels.shape[1]), (0, 0)))
    panels = jnp.transpose(panels.reshape(2, 4, QP, W), (1, 0, 3, 2))
    part = lambda k: lax.dynamic_index_in_dim(panels, (z + k) % 4, 0, keepdims=False)
    pieces = [part(0), shift(part(1), Z, 1), shift(part(3), Z, -1), shift(part(2), Z, 2)]
    left = jnp.stack([piece[0] for piece in pieces])
    right = jnp.stack([piece[1] for piece in pieces])
    amps = over_ring(over_ring(jnp.transpose(amplitudes, (1, 0, 2)), "x"), "y")
    left, right, amps = gate([left, right, amps], [])
    amps = lax.all_gather(amps, ("zh", "zl", "c"), axis=0)
    left_s, right_s = swap(left), swap(right)
    left_1, right_1 = onward(left, "x"), onward(right, "y")
    left_1, right_1, left_s, right_s = gate([left_1, right_1, left_s, right_s], [])
    left_1s, right_1s = onward(left_s, "x"), onward(right_s, "y")
    right_1p = swap(right_1)
    left_1, right_1, left_1s, right_1s = gate([left_1, right_1, left_1s, right_1s], [right_1p])
    left_2, right_2 = onward(left_1, "x"), onward(right_1, "y")
    right_1sp = swap(right_1s)
    near = (right, right_s, right_1, right_1s, right_1p, right_1sp)
    cores = [core, 1 - core, core, 1 - core, 1 - core, core, core, 1 - core]
    back = jnp.where(core == 0, 3, 1)
    ys = [y, (y + back) % 4, (y + 4 - back) % 4, (y + 2) % 4]
    slot_of = [sum(jnp.where(ys[s] == k, s, 0) for s in range(4)) for k in range(4)]
    place = [(z + k) % 4 for k in RING] + cores + slot_of + [(base + k) % 4 for base in (y, x) for k in RING]
    place = jnp.stack(place).astype(jnp.int32)
    xs = near_integrals(place, (left, left_1, left_1s), near)
    right_2, xs = gate([right_2, xs], [])
    far = (right_2, swap(right_2))
    partial = far_ladder(place, xs, (left, left_1, left_1s, left_2), amps, near + far)
    gathered = lax.all_to_all(partial.reshape(32, 16, 256), ("zh", "x", "zl", "c"), 0, 0, tiled=True)
    summed = jnp.sum(gathered.reshape(2, 4, 2, 2, 16, 4, 4, 2, 8).astype(jnp.float32), axis=(0, 2))
    upward = [summed[:, 0][:, :, :, s] for s in (0, 2, 3, 1)]
    downward = [summed[:, 1][:, :, :, s] for s in (0, 1, 3, 2)]
    steps = jnp.stack([jnp.stack([u, d], axis=1) for u, d in zip(upward, downward)])
    steps = lax.dynamic_slice_in_dim(jnp.concatenate([steps, steps]), (4 - y) % 4, 4)
    units = jnp.transpose(steps, (1, 2, 4, 0, 3, 5, 6)).reshape(32, 4, 16, 2, 8)
    block = jnp.take(units, jnp.array(place_units(), jnp.int32), axis=0)
    block = block.reshape(4, 4, 2, 4, 16, 2, 2, 2, 2)
    block = jnp.transpose(block, (4, 1, 5, 2, 3, 6, 0, 7, 8)).reshape(16, 16, W)
    first = lax.dynamic_slice_in_dim(eps_virtual, blocks[0] * W + (y * 2 + zh) * 16, 16)
    second = lax.dynamic_slice_in_dim(eps_virtual, blocks[1] * W, W)
    pairs = lax.dynamic_slice_in_dim(pair_list, ((x * 2 + zl) * 2 + core) * 16, 16, axis=0)
    levels = jnp.arange(eps_occupied.shape[0], dtype=jnp.int32)
    picked = jnp.where(pairs[:, :, None] == levels[None, None, :], eps_occupied[None, None, :], 0.0)
    pair_sum = jnp.sum(picked, axis=(1, 2))
    denominator = first[None, :, None] + second[None, None, :] - pair_sum[:, None, None]
    return (block / denominator).astype(jnp.bfloat16)


def solution(mesh):
    fine = Mesh(mesh.devices.reshape(4, 2, 4, 2, 2), ALL)
    return jax.shard_map(
        shards,
        mesh=fine,
        in_specs=(
            P(None, ALL, None),
            P(None, ALL, None),
            P(("x", "zl", "c"), ("y", "zh"), None),
            P(),
            P(),
            P(),
            P(),
        ),
        out_specs=P(("x", "zl", "c"), ("y", "zh"), None),
        check_vma=False,
    )
```

```python
import jax
import jax.numpy as jnp
import numpy as np
from jax import lax
from jax.experimental import pallas as pl
from jax.experimental.pallas import tpu as pltpu
from jax.sharding import Mesh, PartitionSpec as P

Z = ("zh", "zl")
ALL = ("y", "zh", "x", "zl", "c")
RING = (0, 3, 1, 2)
QP = 1280
W = 128
CC = 16
ROWS1, ROWS2, ROWS3 = 128, 160, 224
FIRST = ((0, 1, 2, 4), (3, 5), (6, 7))
ANYWHERE = pl.BlockSpec(memory_space=pl.ANY)
SCALARS = pl.BlockSpec(memory_space=pltpu.SMEM)
LIMIT = 58 * 2**20


def gate(values, after):
    count = len(values)

    def nothing(*refs):
        pass

    return pl.pallas_call(
        nothing,
        out_shape=[jax.ShapeDtypeStruct(v.shape, v.dtype) for v in values],
        in_specs=[ANYWHERE] * (count + len(after)),
        out_specs=[ANYWHERE] * count,
        input_output_aliases={k: k for k in range(count)},
        name="gate",
    )(*values, *after)


def times(left, right):
    rows = left.shape[0] * W if left.ndim == 3 else left.shape[0] * left.shape[1] * W
    return lax.dot_general(
        left.reshape(rows, QP), right.reshape(4 * W, QP), (((1,), (1,)), ((), ())), preferred_element_type=jnp.float32
    )


def pair_integrals(place, lefts, right, scr, stride, first):
    m = times(lefts, right)
    for u in range(2):
        for za in range(4):
            for zb in range(4):
                row = first + place[12 + za] + u * 8 + place[zb]
                k = u * 4 + za
                scr[pl.ds(row, W, stride=stride), :] = m[k * W : (k + 1) * W, zb * W : (zb + 1) * W]


def single_integrals(place, left, right, core, scr, stride, first):
    m = times(left, right)
    for za in range(4):
        for zb in range(4):
            row = first + place[za] * 8 + place[zb] * 2 + core
            scr[pl.ds(row, W, stride=stride), :] = m[za * W : (za + 1) * W, zb * W : (zb + 1) * W]


def round_out(scr, xbuf, xs, rows, sems):
    quarter = W // 4
    stores = [
        pltpu.make_async_copy(xbuf.at[pl.ds(k * quarter, quarter)], xs.at[pl.ds(k * quarter, quarter)], sems.at[k]) for k in range(4)
    ]
    for k in range(4):

        def convert(c, carry):
            start = pl.multiple_of(c * (rows + 8), 8)
            xbuf[c] = scr[pl.ds(start, rows), :].astype(jnp.bfloat16)
            return carry

        lax.fori_loop(k * quarter, (k + 1) * quarter, convert, 0, unroll=8)
        stores[k].start()
    for store in stores:
        store.wait()


def first_kernel(place, l0, l1, *refs):
    rights, (xs, lbuf, rbuf, scr, xbuf, sems, out_sems) = refs[:4], refs[4:]
    copies = [pltpu.make_async_copy(ref, lbuf.at[u], sems.at[4 + u]) for u, ref in enumerate((l0, l1))]
    copies += [pltpu.make_async_copy(ref, rbuf.at[g], sems.at[g]) for g, ref in enumerate(rights)]
    for copy in copies:
        copy.start()
    for copy in copies[:2]:
        copy.wait()

    def block(g, carry):
        pltpu.make_async_copy(l0, rbuf.at[g], sems.at[g]).wait()
        pair_integrals(place, lbuf[...], rbuf[g], scr, ROWS1 + 8, g * 32)
        return carry

    lax.fori_loop(0, 4, block, 0)
    round_out(scr, xbuf, xs, ROWS1, out_sems)


def second_kernel(place, l0, l1, l2, *refs):
    rights, (xs, lbuf, rbuf, scr, xbuf, sems, out_sems) = refs[:6], refs[6:]
    copies = [pltpu.make_async_copy(ref, lbuf.at[u], sems.at[6 + u]) for u, ref in enumerate((l0, l1, l2))]
    copies += [pltpu.make_async_copy(rights[g], rbuf.at[g], sems.at[g]) for g in (3, 5, 0, 1, 2, 4)]
    for copy in copies:
        copy.start()
    for copy in copies[:5]:
        copy.wait()

    def pairs(k, carry):
        pair_integrals(place, lbuf[:2], rbuf[3 + 2 * k], scr, ROWS2 + 8, k * 32)
        return carry

    lax.fori_loop(0, 2, pairs, 0)
    for copy in copies[5:]:
        copy.wait()

    def singles(g, carry):
        single_integrals(place, lbuf[2], rbuf[g], place[4 + g], scr, ROWS2 + 8, 64 + (g // 2) * 32)
        return carry

    lax.fori_loop(0, 6, singles, 0)
    round_out(scr, xbuf, xs, ROWS2, out_sems)


def integrals(kernel, rows, place, lefts, rights):
    units, count = len(lefts), len(rights)
    return pl.pallas_call(
        kernel,
        out_shape=jax.ShapeDtypeStruct((W, rows, W), jnp.bfloat16),
        in_specs=[SCALARS] + [ANYWHERE] * (units + count),
        out_specs=ANYWHERE,
        scratch_shapes=[
            pltpu.VMEM((units, 4, W, QP), jnp.bfloat16),
            pltpu.VMEM((count, 4, W, QP), jnp.bfloat16),
            pltpu.VMEM((W * (rows + 8), W), jnp.float32),
            pltpu.VMEM((W, rows, W), jnp.bfloat16),
            pltpu.SemaphoreType.DMA((units + count,)),
            pltpu.SemaphoreType.DMA((4,)),
        ],
        compiler_params=pltpu.CompilerParams(vmem_limit_bytes=LIMIT),
        cost_estimate=pl.CostEstimate(flops=10 * 10**9, bytes_accessed=10**7, transcendentals=0),
        name="integrals%d" % units,
    )(place, *lefts, *rights)


def far_kernel(place, x1, x2, l0, l1, l2, l3, amps, *refs):
    rights, (out, lbuf, rbuf, tbuf, xbuf1, xbuf2, scr, acc, sems) = refs[:8], refs[8:]
    copies_l = [pltpu.make_async_copy(ref, lbuf.at[u], sems.at[8 + u]) for u, ref in enumerate((l0, l1, l2, l3))]
    copies_r = [pltpu.make_async_copy(ref, rbuf.at[g], sems.at[g]) for g, ref in enumerate(rights)]
    later = [
        pltpu.make_async_copy(amps, tbuf, sems.at[12]),
        pltpu.make_async_copy(x1, xbuf1, sems.at[13]),
        pltpu.make_async_copy(x2, xbuf2, sems.at[14]),
    ]
    soon = copies_l[:2] + copies_r[6:] + copies_l[2:]
    for copy in soon + copies_r[:6] + later:
        copy.start()
    stride = ROWS3 + 8
    for copy in soon[:4]:
        copy.wait()

    def pairs(k, carry):
        pair_integrals(place, lbuf[:2], rbuf[6 + k], scr, stride, k * 32)
        return carry

    lax.fori_loop(0, 2, pairs, 0)
    for copy in soon[4:]:
        copy.wait()

    def opposite(g, carry):
        single_integrals(place, lbuf[2], rbuf[g], place[4 + g], scr, stride, 64)
        return carry

    lax.fori_loop(6, 8, opposite, 0)

    def last(g, carry):
        @pl.when(g < 6)
        def _():
            pltpu.make_async_copy(l0, rbuf.at[g], sems.at[g]).wait()

        single_integrals(place, lbuf[3], rbuf[g], place[4 + g], scr, stride, 96 + (g // 2) * 32)
        return carry

    lax.fori_loop(0, 8, last, 0)
    for copy in later:
        copy.wait()
    acc[...] = jnp.zeros_like(acc)

    def contract(step, carry):
        x = []
        t = []
        for k in range(CC):
            c = step * CC + k
            groups = []
            for values in (
                xbuf1[c],
                xbuf2[c],
                scr[pl.ds(pl.multiple_of(c * stride, 8), ROWS3), :].astype(jnp.bfloat16),
            ):
                groups += [values[g * 32 : g * 32 + 32] for g in range(values.shape[0] // 32)]
            x.append(jnp.concatenate([group[zh * 16 : zh * 16 + 16] for zh in range(2) for group in groups], axis=0))
            y, zh, low = c // 32, (c // 16) % 2, c % 16
            t.append(
                jnp.concatenate(
                    [tbuf[(zh * 2 + zl) * 2 + core, y, xx, low] for xx in range(4) for zl in range(2) for core in range(2)],
                    axis=0,
                )
            )
        acc[...] += lax.dot_general(
            jnp.concatenate(t, axis=1),
            jnp.concatenate(x, axis=1),
            (((1,), (1,)), ((), ())),
            preferred_element_type=jnp.float32,
        )
        return carry

    lax.fori_loop(0, W // CC, contract, 0)
    for zh in range(2):
        out[zh] = acc[:, zh * 256 : (zh + 1) * 256].astype(out.dtype).reshape(16, 16, 256)


def far_ladder(place, x1, x2, lefts, amps, rights):
    return pl.pallas_call(
        far_kernel,
        out_shape=jax.ShapeDtypeStruct((2, 16, 16, 256), jnp.bfloat16),
        in_specs=[SCALARS] + [ANYWHERE] * 15,
        out_specs=pl.BlockSpec(memory_space=pltpu.VMEM),
        scratch_shapes=[
            pltpu.VMEM((4, 4, W, QP), jnp.bfloat16),
            pltpu.VMEM((8, 4, W, QP), jnp.bfloat16),
            pltpu.VMEM((8, 4, 4, 16, 16, W), jnp.bfloat16),
            pltpu.VMEM((W, ROWS1, W), jnp.bfloat16),
            pltpu.VMEM((W, ROWS2, W), jnp.bfloat16),
            pltpu.VMEM((W * (ROWS3 + 8), W), jnp.float32),
            pltpu.VMEM((256, 512), jnp.float32),
            pltpu.SemaphoreType.DMA((15,)),
        ],
        compiler_params=pltpu.CompilerParams(vmem_limit_bytes=LIMIT),
        cost_estimate=pl.CostEstimate(flops=15 * 10**9, bytes_accessed=10**7, transcendentals=0),
        name="far_ladder",
    )(place, x1, x2, *lefts, amps, *rights)


def swap(value):
    return lax.ppermute(value, "c", [(0, 1), (1, 0)])


def shift(value, axis, step):
    return lax.ppermute(value, axis, [(i, (i + step) % 4) for i in range(4)])


def onward(value, axis):
    pairs = [(i * 2 + c, (i + 1 - 2 * c) % 4 * 2 + c) for i in range(4) for c in range(2)]
    return lax.ppermute(value, (axis, "c"), pairs)


def lane_table():
    table = np.full((4, 4, 2, 512), -1, np.int32)
    group_of = {block: k for k, block in enumerate(FIRST[0])}
    group_of.update({FIRST[1][k]: 4 + k for k in range(2)})
    group_of.update({FIRST[2][k]: 9 + k for k in range(2)})
    for y, x, far, zl, c, yb, zb, cb in np.ndindex(4, 4, 4, 2, 2, 4, 4, 2):
        step = (far - x) % 4
        if step in (0, 2):
            core, unit = c, (0 if step == 0 else 3)
        else:
            core = 0 if step == 3 else 1
            unit = 1 if core == c else 2
        slot = ({0: 0, 3: 1, 1: 2, 2: 3} if core == 0 else {0: 0, 1: 1, 3: 2, 2: 3})[(yb - y) % 4]
        own = (cb == core) != (slot == 2)
        if unit < 2:
            lane = group_of[slot * 2 + (0 if own else 1)] * 16 + unit * 8 + zl * 4 + zb
        else:
            group = (6, 7, 8, 11)[slot] if unit == 2 else 12 + slot
            lane = group * 16 + zl * 8 + zb * 2 + cb
        table[y, x, core, ((far * 2 + zl) * 2 + c) * 32 + (yb * 4 + zb) * 2 + cb] = lane
    return table


def shards(panel_left, panel_right, amplitudes, eps_virtual, eps_occupied, pair_list, blocks):
    y, zh, x, zl, core = (lax.axis_index(name) for name in ALL)
    z = zh * 2 + zl
    panels = jnp.stack([panel_left[:, 0, :], panel_right[:, 0, :]])
    panels = jnp.pad(panels, ((0, 0), (0, 4 * QP - panels.shape[1]), (0, 0)))
    panels = jnp.transpose(panels.reshape(2, 4, QP, W), (1, 0, 3, 2))
    part = lambda k: lax.dynamic_index_in_dim(panels, (z + k) % 4, 0, keepdims=False)
    near_z = [shift(part(1), Z, 1), shift(part(3), Z, -1)]
    amps = lax.all_gather(jnp.transpose(amplitudes, (1, 0, 2)), "x", axis=0)
    opposite = gate([part(2)], near_z)[0]
    pieces = [part(0)] + near_z + [shift(opposite, Z, 2)]
    amps = lax.all_gather(amps, "y", axis=0)
    left = jnp.stack([piece[0] for piece in pieces])
    right = jnp.stack([piece[1] for piece in pieces])
    left_s, right_s = swap(left), swap(right)
    amps = lax.all_gather(gate([amps], [left_s, right_s])[0], ("zh", "zl", "c"), axis=0)
    left_1, right_1 = onward(left, "x"), onward(right, "y")
    left_1s, right_1s = onward(left_s, "x"), onward(right_s, "y")
    right_1p = swap(right_1)
    left_2, right_2 = onward(left_1, "x"), onward(right_1, "y")
    cores = [core, 1 - core, core, 1 - core, 1 - core, core, core, 1 - core]
    zs = [(z + k) % 4 for k in RING]
    place = jnp.stack(zs + cores + [(k // 2) * 16 + (k % 2) * 4 for k in zs]).astype(jnp.int32)
    x1 = integrals(first_kernel, ROWS1, place, (left, left_1), (right, right_s, right_1, right_1p))
    right_1s = gate([right_1s], [x1])[0]
    rights = (right, right_s, right_1, right_1s, right_1p, swap(right_1s))
    x2 = integrals(second_kernel, ROWS2, place, (left, left_1, left_1s), rights)
    right_2, x2 = gate([right_2, x2], [])
    rights = rights + (right_2, swap(right_2))
    partial = far_ladder(place, x1, x2, (left, left_1, left_1s, left_2), amps, rights)
    gathered = lax.all_to_all(partial.reshape(32, 16, 256), ("zh", "x", "zl", "c"), 0, 0, tiled=True)
    lanes = lax.dynamic_index_in_dim(jnp.array(lane_table()), y, 0, keepdims=False)
    pick = (lanes[:, :, None, :] == jnp.arange(256, dtype=jnp.int32)[None, None, :, None]).astype(jnp.bfloat16)
    parts = jnp.einsum("hxlkpj,xkjm->hlxpm", gathered.reshape(2, 4, 2, 2, 16, 256), pick, preferred_element_type=jnp.float32)
    block = jnp.sum(parts, axis=(0, 1)).reshape(4, 16, 16, 8, 4)
    block = jnp.transpose(block, (1, 2, 3, 0, 4)).reshape(16, 16, W)
    first = lax.dynamic_slice_in_dim(eps_virtual, blocks[0] * W + (y * 2 + zh) * 16, 16)
    second = lax.dynamic_slice_in_dim(eps_virtual, blocks[1] * W, W)
    pairs = lax.dynamic_slice_in_dim(pair_list, ((x * 2 + zl) * 2 + core) * 16, 16, axis=0)
    levels = jnp.arange(eps_occupied.shape[0], dtype=jnp.int32)
    picked = jnp.where(pairs[:, :, None] == levels[None, None, :], eps_occupied[None, None, :], 0.0)
    pair_sum = jnp.sum(picked, axis=(1, 2))
    denominator = first[None, :, None] + second[None, None, :] - pair_sum[:, None, None]
    return (block / denominator).astype(jnp.bfloat16)


def solution(mesh):
    fine = Mesh(mesh.devices.reshape(4, 2, 4, 2, 2), ALL)
    return jax.shard_map(
        shards,
        mesh=fine,
        in_specs=(
            P(None, ALL, None),
            P(None, ALL, None),
            P(("x", "zl", "c"), ("y", "zh"), None),
            P(),
            P(),
            P(),
            P(),
        ),
        out_specs=P(("x", "zl", "c"), ("y", "zh"), None),
        check_vma=False,
    )
```

```python
import jax
import jax.numpy as jnp
import numpy as np
from jax import lax
from jax.experimental import pallas as pl
from jax.experimental.pallas import tpu as pltpu
from jax.sharding import Mesh, PartitionSpec as P

Z = ("zh", "zl")
ALL = ("y", "zh", "x", "zl", "c")
RING = (0, 3, 1, 2)
QP = 1280
W = 128
CC = 16
ROWS1, ROWS2, ROWS3 = 96, 192, 224
FIRST = ((0, 1, 2), (3, 4, 5), (6, 7))
ANYWHERE = pl.BlockSpec(memory_space=pl.ANY)
SCALARS = pl.BlockSpec(memory_space=pltpu.SMEM)
LIMIT = 50 * 2**20


def gate(values, after):
    count = len(values)

    def nothing(*refs):
        pass

    return pl.pallas_call(
        nothing,
        out_shape=[jax.ShapeDtypeStruct(v.shape, v.dtype) for v in values],
        in_specs=[ANYWHERE] * (count + len(after)),
        out_specs=[ANYWHERE] * count,
        input_output_aliases={k: k for k in range(count)},
        compiler_params=pltpu.CompilerParams(vmem_limit_bytes=2**20),
        name="gate",
    )(*values, *after)


def times(left, right):
    rows = left.shape[0] * W if left.ndim == 3 else left.shape[0] * left.shape[1] * W
    return lax.dot_general(
        left.reshape(rows, QP), right.reshape(4 * W, QP), (((1,), (1,)), ((), ())), preferred_element_type=jnp.float32
    )


def pair_integrals(place, lefts, right, scr, stride, first):
    m = times(lefts, right)
    for u in range(2):
        for za in range(4):
            for zb in range(4):
                row = first + place[12 + za] + u * 8 + place[zb]
                k = u * 4 + za
                scr[pl.ds(row, W, stride=stride), :] = m[k * W : (k + 1) * W, zb * W : (zb + 1) * W]


def single_integrals(place, left, right, core, scr, stride, first):
    m = times(left, right)
    for za in range(4):
        for zb in range(4):
            row = first + place[za] * 8 + place[zb] * 2 + core
            scr[pl.ds(row, W, stride=stride), :] = m[za * W : (za + 1) * W, zb * W : (zb + 1) * W]


def round_out(scr, xbuf, xs, rows, sems):
    quarter = W // 4
    stores = [
        pltpu.make_async_copy(xbuf.at[pl.ds(k * quarter, quarter)], xs.at[pl.ds(k * quarter, quarter)], sems.at[k]) for k in range(4)
    ]
    for k in range(4):

        def convert(c, carry):
            start = pl.multiple_of(c * (rows + 8), 8)
            xbuf[c] = scr[pl.ds(start, rows), :].astype(jnp.bfloat16)
            return carry

        lax.fori_loop(k * quarter, (k + 1) * quarter, convert, 0, unroll=8)
        stores[k].start()
    for store in stores:
        store.wait()


def first_kernel(place, l0, l1, *refs):
    rights, (xs, lbuf, rbuf, scr, xbuf, sems, out_sems) = refs[:3], refs[3:]
    copies = [pltpu.make_async_copy(ref, lbuf.at[u], sems.at[3 + u]) for u, ref in enumerate((l0, l1))]
    copies += [pltpu.make_async_copy(ref, rbuf.at[g], sems.at[g]) for g, ref in enumerate(rights)]
    for copy in copies:
        copy.start()
    for copy in copies[:2]:
        copy.wait()

    def block(g, carry):
        pltpu.make_async_copy(l0, rbuf.at[g], sems.at[g]).wait()
        pair_integrals(place, lbuf[...], rbuf[g], scr, ROWS1 + 8, g * 32)
        return carry

    lax.fori_loop(0, 3, block, 0)
    round_out(scr, xbuf, xs, ROWS1, out_sems)


def second_kernel(place, l0, l1, l2, *refs):
    rights, (xs, lbuf, rbuf, scr, xbuf, sems, out_sems) = refs[:6], refs[6:]
    copies = [pltpu.make_async_copy(ref, lbuf.at[u], sems.at[6 + u]) for u, ref in enumerate((l0, l1, l2))]
    copies += [pltpu.make_async_copy(rights[g], rbuf.at[g], sems.at[g]) for g in (3, 4, 5, 0, 1, 2)]
    for copy in copies:
        copy.start()
    for copy in copies[:6]:
        copy.wait()

    def pairs(k, carry):
        pair_integrals(place, lbuf[:2], rbuf[3 + k], scr, ROWS2 + 8, k * 32)
        return carry

    lax.fori_loop(0, 3, pairs, 0)
    for copy in copies[6:]:
        copy.wait()

    def singles(g, carry):
        single_integrals(place, lbuf[2], rbuf[g], place[4 + g], scr, ROWS2 + 8, 96 + (g // 2) * 32)
        return carry

    lax.fori_loop(0, 6, singles, 0)
    round_out(scr, xbuf, xs, ROWS2, out_sems)


def integrals(kernel, rows, place, lefts, rights):
    units, count = len(lefts), len(rights)
    return pl.pallas_call(
        kernel,
        out_shape=jax.ShapeDtypeStruct((W, rows, W), jnp.bfloat16),
        in_specs=[SCALARS] + [ANYWHERE] * (units + count),
        out_specs=pl.BlockSpec(memory_space=pltpu.HBM),
        scratch_shapes=[
            pltpu.VMEM((units, 4, W, QP), jnp.bfloat16),
            pltpu.VMEM((count, 4, W, QP), jnp.bfloat16),
            pltpu.VMEM((W * (rows + 8), W), jnp.float32),
            pltpu.VMEM((W, rows, W), jnp.bfloat16),
            pltpu.SemaphoreType.DMA((units + count,)),
            pltpu.SemaphoreType.DMA((4,)),
        ],
        compiler_params=pltpu.CompilerParams(vmem_limit_bytes=(26 if units == 2 else 34) * 2**20),
        cost_estimate=pl.CostEstimate(flops=10**6, bytes_accessed=10**4, transcendentals=0),
        name="integrals%d" % units,
    )(place, *lefts, *rights)


def far_kernel(place, x1, x2, l0, l1, l2, l3, amps, *refs):
    rights, (out, lbuf, rbuf, tbuf, xbuf1, xbuf2, scr, acc, sems) = refs[:8], refs[8:]
    copies_l = [pltpu.make_async_copy(ref, lbuf.at[u], sems.at[8 + u]) for u, ref in enumerate((l0, l1, l2, l3))]
    copies_r = [pltpu.make_async_copy(ref, rbuf.at[g], sems.at[g]) for g, ref in enumerate(rights)]
    later = [
        pltpu.make_async_copy(amps, tbuf, sems.at[12]),
        pltpu.make_async_copy(x1, xbuf1, sems.at[13]),
        pltpu.make_async_copy(x2, xbuf2, sems.at[14]),
    ]
    soon = copies_l[:2] + copies_r[6:] + copies_l[2:]
    for copy in soon + copies_r[:6] + later:
        copy.start()
    stride = ROWS3 + 8
    for copy in soon[:4]:
        copy.wait()

    def pairs(k, carry):
        pair_integrals(place, lbuf[:2], rbuf[6 + k], scr, stride, k * 32)
        return carry

    lax.fori_loop(0, 2, pairs, 0)
    for copy in soon[4:]:
        copy.wait()

    def opposite(g, carry):
        single_integrals(place, lbuf[2], rbuf[g], place[4 + g], scr, stride, 64)
        return carry

    lax.fori_loop(6, 8, opposite, 0)

    def last(g, carry):
        @pl.when(g < 6)
        def _():
            pltpu.make_async_copy(l0, rbuf.at[g], sems.at[g]).wait()

        single_integrals(place, lbuf[3], rbuf[g], place[4 + g], scr, stride, 96 + (g // 2) * 32)
        return carry

    lax.fori_loop(0, 8, last, 0)
    for copy in later:
        copy.wait()
    acc[...] = jnp.zeros_like(acc)

    def contract(step, carry):
        x = []
        t = []
        for k in range(CC):
            c = step * CC + k
            groups = []
            for values in (
                xbuf1[c],
                xbuf2[c],
                scr[pl.ds(pl.multiple_of(c * stride, 8), ROWS3), :].astype(jnp.bfloat16),
            ):
                groups += [values[g * 32 : g * 32 + 32] for g in range(values.shape[0] // 32)]
            x.append(jnp.concatenate([group[zh * 16 : zh * 16 + 16] for zh in range(2) for group in groups], axis=0))
            y, zh, low = c // 32, (c // 16) % 2, c % 16
            t.append(
                jnp.concatenate(
                    [tbuf[(zh * 2 + zl) * 2 + core, y, xx, low] for xx in range(4) for zl in range(2) for core in range(2)],
                    axis=0,
                )
            )
        acc[...] += lax.dot_general(
            jnp.concatenate(t, axis=1),
            jnp.concatenate(x, axis=1),
            (((1,), (1,)), ((), ())),
            preferred_element_type=jnp.float32,
        )
        return carry

    lax.fori_loop(0, W // CC, contract, 0)
    for zh in range(2):
        out[zh] = acc[:, zh * 256 : (zh + 1) * 256].astype(out.dtype).reshape(16, 16, 256)


def far_ladder(place, x1, x2, lefts, amps, rights):
    return pl.pallas_call(
        far_kernel,
        out_shape=jax.ShapeDtypeStruct((2, 16, 16, 256), jnp.bfloat16),
        in_specs=[SCALARS] + [ANYWHERE] * 15,
        out_specs=pl.BlockSpec(memory_space=pltpu.VMEM),
        scratch_shapes=[
            pltpu.VMEM((4, 4, W, QP), jnp.bfloat16),
            pltpu.VMEM((8, 4, W, QP), jnp.bfloat16),
            pltpu.VMEM((8, 4, 4, 16, 16, W), jnp.bfloat16),
            pltpu.VMEM((W, ROWS1, W), jnp.bfloat16),
            pltpu.VMEM((W, ROWS2, W), jnp.bfloat16),
            pltpu.VMEM((W * (ROWS3 + 8), W), jnp.float32),
            pltpu.VMEM((256, 512), jnp.float32),
            pltpu.SemaphoreType.DMA((15,)),
        ],
        compiler_params=pltpu.CompilerParams(vmem_limit_bytes=LIMIT),
        cost_estimate=pl.CostEstimate(flops=15 * 10**9, bytes_accessed=10**7, transcendentals=0),
        name="far_ladder",
    )(place, x1, x2, *lefts, amps, *rights)


def swap(value):
    return lax.ppermute(value, "c", [(0, 1), (1, 0)])


def shift(value, axis, step):
    return lax.ppermute(value, axis, [(i, (i + step) % 4) for i in range(4)])


def onward(value, axis):
    pairs = [(i * 2 + c, (i + 1 - 2 * c) % 4 * 2 + c) for i in range(4) for c in range(2)]
    return lax.ppermute(value, (axis, "c"), pairs)


def lane_table():
    table = np.full((4, 4, 2, 512), -1, np.int32)
    group_of = {block: k for k, block in enumerate(FIRST[0])}
    group_of.update({FIRST[1][k]: 3 + k for k in range(3)})
    group_of.update({FIRST[2][k]: 9 + k for k in range(2)})
    for y, x, far, zl, c, yb, zb, cb in np.ndindex(4, 4, 4, 2, 2, 4, 4, 2):
        step = (far - x) % 4
        if step in (0, 2):
            core, unit = c, (0 if step == 0 else 3)
        else:
            core = 0 if step == 3 else 1
            unit = 1 if core == c else 2
        slot = ({0: 0, 3: 1, 1: 2, 2: 3} if core == 0 else {0: 0, 1: 1, 3: 2, 2: 3})[(yb - y) % 4]
        own = (cb == core) != (slot == 2)
        if unit < 2:
            lane = group_of[slot * 2 + (0 if own else 1)] * 16 + unit * 8 + zl * 4 + zb
        else:
            group = (6, 7, 8, 11)[slot] if unit == 2 else 12 + slot
            lane = group * 16 + zl * 8 + zb * 2 + cb
        table[y, x, core, ((far * 2 + zl) * 2 + c) * 32 + (yb * 4 + zb) * 2 + cb] = lane
    return table


def shards(panel_left, panel_right, amplitudes, eps_virtual, eps_occupied, pair_list, blocks):
    y, zh, x, zl, core = (lax.axis_index(name) for name in ALL)
    z = zh * 2 + zl
    panels = jnp.stack([panel_left[:, 0, :], panel_right[:, 0, :]])
    panels = jnp.pad(panels, ((0, 0), (0, 4 * QP - panels.shape[1]), (0, 0)))
    panels = jnp.transpose(panels.reshape(2, 4, QP, W), (1, 0, 3, 2))
    part = lambda k: lax.dynamic_index_in_dim(panels, (z + k) % 4, 0, keepdims=False)
    near_z = [shift(part(1), Z, 1), shift(part(3), Z, -1)]
    amps = lax.all_gather(jnp.transpose(amplitudes, (1, 0, 2)), "x", axis=0)
    opposite = gate([part(2)], near_z)[0]
    pieces = [part(0)] + near_z + [shift(opposite, Z, 2)]
    amps = lax.all_gather(amps, "y", axis=0)
    left = jnp.stack([piece[0] for piece in pieces])
    right = jnp.stack([piece[1] for piece in pieces])
    left_s, right_s = swap(left), swap(right)
    amps = lax.all_gather(gate([amps], [left_s, right_s])[0], ("zh", "zl", "c"), axis=0)
    left_1, right_1 = onward(left, "x"), onward(right, "y")
    left_1s, right_1s = onward(left_s, "x"), onward(right_s, "y")
    right_1p = swap(right_1)
    left_2, right_2 = onward(left_1, "x"), onward(right_1, "y")
    cores = [core, 1 - core, core, 1 - core, 1 - core, core, core, 1 - core]
    zs = [(z + k) % 4 for k in RING]
    place = jnp.stack(zs + cores + [(k // 2) * 16 + (k % 2) * 4 for k in zs]).astype(jnp.int32)
    x1 = integrals(first_kernel, ROWS1, place, (left, left_1), (right, right_s, right_1))
    right_1s = gate([right_1s], [x1])[0]
    rights = (right, right_s, right_1, right_1s, right_1p, swap(right_1s))
    x2 = integrals(second_kernel, ROWS2, place, (left, left_1, left_1s), rights)
    right_2 = gate([right_2], [x2])[0]
    rights = rights + (right_2, swap(right_2))
    partial = far_ladder(place, x1, x2, (left, left_1, left_1s, left_2), amps, rights)
    gathered = lax.all_to_all(partial.reshape(32, 16, 256), ("zh", "x", "zl", "c"), 0, 0, tiled=True)
    lanes = lax.dynamic_index_in_dim(jnp.array(lane_table()), y, 0, keepdims=False)
    pick = (lanes[:, :, None, :] == jnp.arange(256, dtype=jnp.int32)[None, None, :, None]).astype(jnp.bfloat16)
    parts = jnp.einsum("hxlkpj,xkjm->hlxpm", gathered.reshape(2, 4, 2, 2, 16, 256), pick, preferred_element_type=jnp.float32)
    block = jnp.sum(parts, axis=(0, 1)).reshape(4, 16, 16, 8, 4)
    block = jnp.transpose(block, (1, 2, 3, 0, 4)).reshape(16, 16, W)
    first = lax.dynamic_slice_in_dim(eps_virtual, blocks[0] * W + (y * 2 + zh) * 16, 16)
    second = lax.dynamic_slice_in_dim(eps_virtual, blocks[1] * W, W)
    pairs = lax.dynamic_slice_in_dim(pair_list, ((x * 2 + zl) * 2 + core) * 16, 16, axis=0)
    levels = jnp.arange(eps_occupied.shape[0], dtype=jnp.int32)
    picked = jnp.where(pairs[:, :, None] == levels[None, None, :], eps_occupied[None, None, :], 0.0)
    pair_sum = jnp.sum(picked, axis=(1, 2))
    denominator = first[None, :, None] + second[None, None, :] - pair_sum[:, None, None]
    return (block / denominator).astype(jnp.bfloat16)


def solution(mesh):
    fine = Mesh(mesh.devices.reshape(4, 2, 4, 2, 2), ALL)
    return jax.shard_map(
        shards,
        mesh=fine,
        in_specs=(
            P(None, ALL, None),
            P(None, ALL, None),
            P(("x", "zl", "c"), ("y", "zh"), None),
            P(),
            P(),
            P(),
            P(),
        ),
        out_specs=P(("x", "zl", "c"), ("y", "zh"), None),
        check_vma=False,
    )
```

```python
import jax
import jax.numpy as jnp
import numpy as np
from jax import lax
from jax.experimental import pallas as pl
from jax.experimental.pallas import tpu as pltpu
from jax.sharding import Mesh, PartitionSpec as P

Z = ("zh", "zl")
ALL = ("y", "zh", "x", "zl", "c")
RING = (0, 3, 1, 2)
QP = 1280
W = 128
CC = 32
ROWS1, ROWS2, ROWS3 = 96, 192, 224
FIRST = ((0, 1, 2), (3, 4, 5), (6, 7))
ANYWHERE = pl.BlockSpec(memory_space=pl.ANY)
SCALARS = pl.BlockSpec(memory_space=pltpu.SMEM)
LIMIT = 55 * 2**20


def gate(values, after, limit=2**20):
    count = len(values)

    def nothing(*refs):
        pass

    return pl.pallas_call(
        nothing,
        out_shape=[jax.ShapeDtypeStruct(v.shape, v.dtype) for v in values],
        in_specs=[ANYWHERE] * (count + len(after)),
        out_specs=[ANYWHERE] * count,
        input_output_aliases={k: k for k in range(count)},
        compiler_params=pltpu.CompilerParams(vmem_limit_bytes=limit),
        name="gate",
    )(*values, *after)


def times(left, right):
    rows = left.shape[0] * W if left.ndim == 3 else left.shape[0] * left.shape[1] * W
    return lax.dot_general(
        left.reshape(rows, QP), right.reshape(4 * W, QP), (((1,), (1,)), ((), ())), preferred_element_type=jnp.float32
    )


def pair_integrals(place, lefts, right, scr, stride, first):
    m = times(lefts, right)
    for u in range(2):
        for za in range(4):
            for zb in range(4):
                row = first + place[12 + za] + u * 8 + place[zb]
                k = u * 4 + za
                scr[pl.ds(row, W, stride=stride), :] = m[k * W : (k + 1) * W, zb * W : (zb + 1) * W]


def single_integrals(place, left, right, core, scr, stride, first):
    m = times(left, right)
    for za in range(4):
        for zb in range(4):
            row = first + place[za] * 8 + place[zb] * 2 + core
            scr[pl.ds(row, W, stride=stride), :] = m[za * W : (za + 1) * W, zb * W : (zb + 1) * W]


def round_out(scr, xbuf, xs, rows, sems):
    quarter = W // 4
    stores = [
        pltpu.make_async_copy(xbuf.at[pl.ds(k * quarter, quarter)], xs.at[pl.ds(k * quarter, quarter)], sems.at[k]) for k in range(4)
    ]
    for k in range(4):

        def convert(c, carry):
            start = pl.multiple_of(c * (rows + 8), 8)
            xbuf[c] = scr[pl.ds(start, rows), :].astype(jnp.bfloat16)
            return carry

        lax.fori_loop(k * quarter, (k + 1) * quarter, convert, 0, unroll=8)
        stores[k].start()
    for store in stores:
        store.wait()


def first_kernel(place, l0, l1, *refs):
    rights, (xs, lbuf, rbuf, scr, xbuf, sems, out_sems) = refs[:3], refs[3:]
    copies = [pltpu.make_async_copy(ref, lbuf.at[u], sems.at[3 + u]) for u, ref in enumerate((l0, l1))]
    copies += [pltpu.make_async_copy(ref, rbuf.at[g], sems.at[g]) for g, ref in enumerate(rights)]
    for copy in copies:
        copy.start()
    for copy in copies[:2]:
        copy.wait()

    def block(g, carry):
        pltpu.make_async_copy(l0, rbuf.at[g], sems.at[g]).wait()
        pair_integrals(place, lbuf[...], rbuf[g], scr, ROWS1 + 8, g * 32)
        return carry

    lax.fori_loop(0, 3, block, 0)
    round_out(scr, xbuf, xs, ROWS1, out_sems)


def second_kernel(place, l0, l1, l2, *refs):
    rights, (xs, lbuf, rbuf, scr, xbuf, sems, out_sems) = refs[:6], refs[6:]
    copies = [pltpu.make_async_copy(ref, lbuf.at[u], sems.at[6 + u]) for u, ref in enumerate((l0, l1, l2))]
    copies += [pltpu.make_async_copy(rights[g], rbuf.at[g], sems.at[g]) for g in (3, 4, 5, 0, 1, 2)]
    for copy in copies:
        copy.start()
    for copy in copies[:6]:
        copy.wait()

    def pairs(k, carry):
        pair_integrals(place, lbuf[:2], rbuf[3 + k], scr, ROWS2 + 8, k * 32)
        return carry

    lax.fori_loop(0, 3, pairs, 0)
    for copy in copies[6:]:
        copy.wait()

    def singles(g, carry):
        single_integrals(place, lbuf[2], rbuf[g], place[4 + g], scr, ROWS2 + 8, 96 + (g // 2) * 32)
        return carry

    lax.fori_loop(0, 6, singles, 0)
    round_out(scr, xbuf, xs, ROWS2, out_sems)


def integrals(kernel, rows, place, lefts, rights):
    units, count = len(lefts), len(rights)
    return pl.pallas_call(
        kernel,
        out_shape=jax.ShapeDtypeStruct((W, rows, W), jnp.bfloat16),
        in_specs=[SCALARS] + [ANYWHERE] * (units + count),
        out_specs=pl.BlockSpec(memory_space=pltpu.HBM),
        scratch_shapes=[
            pltpu.VMEM((units, 4, W, QP), jnp.bfloat16),
            pltpu.VMEM((count, 4, W, QP), jnp.bfloat16),
            pltpu.VMEM((W * (rows + 8), W), jnp.float32),
            pltpu.VMEM((W, rows, W), jnp.bfloat16),
            pltpu.SemaphoreType.DMA((units + count,)),
            pltpu.SemaphoreType.DMA((4,)),
        ],
        compiler_params=pltpu.CompilerParams(vmem_limit_bytes=(26 if units == 2 else 34) * 2**20),
        cost_estimate=pl.CostEstimate(flops=10**6, bytes_accessed=10**4, transcendentals=0),
        name="integrals%d" % units,
    )(place, *lefts, *rights)


def far_kernel(place, x1, x2, l0, l1, l2, l3, amps, *refs):
    rights, (out, lbuf, rbuf, tbuf, xbuf1, xbuf2, scr, acc, sems) = refs[:8], refs[8:]
    copies_l = [pltpu.make_async_copy(ref, lbuf.at[u], sems.at[8 + u]) for u, ref in enumerate((l0, l1, l2, l3))]
    copies_r = [pltpu.make_async_copy(ref, rbuf.at[g], sems.at[g]) for g, ref in enumerate(rights)]
    later = [
        pltpu.make_async_copy(amps, tbuf, sems.at[12]),
        pltpu.make_async_copy(x1, xbuf1, sems.at[13]),
        pltpu.make_async_copy(x2, xbuf2, sems.at[14]),
    ]
    soon = copies_l[:2] + copies_r[6:] + copies_l[2:]
    for copy in soon + copies_r[:6] + later:
        copy.start()
    stride = ROWS3 + 8
    for copy in soon[:4]:
        copy.wait()

    def pairs(k, carry):
        pair_integrals(place, lbuf[:2], rbuf[6 + k], scr, stride, k * 32)
        return carry

    lax.fori_loop(0, 2, pairs, 0)
    for copy in soon[4:]:
        copy.wait()

    def opposite(g, carry):
        single_integrals(place, lbuf[2], rbuf[g], place[4 + g], scr, stride, 64)
        return carry

    lax.fori_loop(6, 8, opposite, 0)

    def last(g, carry):
        @pl.when(g < 6)
        def _():
            pltpu.make_async_copy(l0, rbuf.at[g], sems.at[g]).wait()

        single_integrals(place, lbuf[3], rbuf[g], place[4 + g], scr, stride, 96 + (g // 2) * 32)
        return carry

    lax.fori_loop(0, 8, last, 0)
    for copy in later:
        copy.wait()
    acc[...] = jnp.zeros_like(acc)

    def contract(step, carry):
        x = []
        t = []
        for k in range(CC):
            c = step * CC + k
            groups = []
            for values in (
                xbuf1[c],
                xbuf2[c],
                scr[pl.ds(pl.multiple_of(c * stride, 8), ROWS3), :].astype(jnp.bfloat16),
            ):
                groups += [values[g * 32 : g * 32 + 32] for g in range(values.shape[0] // 32)]
            x.append(jnp.concatenate([group[zh * 16 : zh * 16 + 16] for zh in range(2) for group in groups], axis=0))
            y, zh, low = c // 32, (c // 16) % 2, c % 16
            t.append(
                jnp.concatenate(
                    [tbuf[(zh * 2 + zl) * 2 + core, y, xx, low] for xx in range(4) for zl in range(2) for core in range(2)],
                    axis=0,
                )
            )
        acc[...] += lax.dot_general(
            jnp.concatenate(t, axis=1),
            jnp.concatenate(x, axis=1),
            (((1,), (1,)), ((), ())),
            preferred_element_type=jnp.float32,
        )
        return carry

    lax.fori_loop(0, W // CC, contract, 0)
    for zh in range(2):
        out[zh] = acc[:, zh * 256 : (zh + 1) * 256].astype(out.dtype).reshape(16, 16, 256)


def far_ladder(place, x1, x2, lefts, amps, rights):
    return pl.pallas_call(
        far_kernel,
        out_shape=jax.ShapeDtypeStruct((2, 16, 16, 256), jnp.bfloat16),
        in_specs=[SCALARS] + [ANYWHERE] * 15,
        out_specs=pl.BlockSpec(memory_space=pltpu.VMEM),
        scratch_shapes=[
            pltpu.VMEM((4, 4, W, QP), jnp.bfloat16),
            pltpu.VMEM((8, 4, W, QP), jnp.bfloat16),
            pltpu.VMEM((8, 4, 4, 16, 16, W), jnp.bfloat16),
            pltpu.VMEM((W, ROWS1, W), jnp.bfloat16),
            pltpu.VMEM((W, ROWS2, W), jnp.bfloat16),
            pltpu.VMEM((W * (ROWS3 + 8), W), jnp.float32),
            pltpu.VMEM((256, 512), jnp.float32),
            pltpu.SemaphoreType.DMA((15,)),
        ],
        compiler_params=pltpu.CompilerParams(vmem_limit_bytes=LIMIT),
        cost_estimate=pl.CostEstimate(flops=15 * 10**9, bytes_accessed=10**7, transcendentals=0),
        name="far_ladder",
    )(place, x1, x2, *lefts, amps, *rights)


def swap(value):
    return lax.ppermute(value, "c", [(0, 1), (1, 0)])


def shift(value, axis, step):
    return lax.ppermute(value, axis, [(i, (i + step) % 4) for i in range(4)])


def onward(value, axis):
    pairs = [(i * 2 + c, (i + 1 - 2 * c) % 4 * 2 + c) for i in range(4) for c in range(2)]
    return lax.ppermute(value, (axis, "c"), pairs)


def lane_table():
    table = np.full((4, 4, 2, 512), -1, np.int32)
    group_of = {block: k for k, block in enumerate(FIRST[0])}
    group_of.update({FIRST[1][k]: 3 + k for k in range(3)})
    group_of.update({FIRST[2][k]: 9 + k for k in range(2)})
    for y, x, far, zl, c, yb, zb, cb in np.ndindex(4, 4, 4, 2, 2, 4, 4, 2):
        step = (far - x) % 4
        if step in (0, 2):
            core, unit = c, (0 if step == 0 else 3)
        else:
            core = 0 if step == 3 else 1
            unit = 1 if core == c else 2
        slot = ({0: 0, 3: 1, 1: 2, 2: 3} if core == 0 else {0: 0, 1: 1, 3: 2, 2: 3})[(yb - y) % 4]
        own = (cb == core) != (slot == 2)
        if unit < 2:
            lane = group_of[slot * 2 + (0 if own else 1)] * 16 + unit * 8 + zl * 4 + zb
        else:
            group = (6, 7, 8, 11)[slot] if unit == 2 else 12 + slot
            lane = group * 16 + zl * 8 + zb * 2 + cb
        table[y, x, core, ((far * 2 + zl) * 2 + c) * 32 + (yb * 4 + zb) * 2 + cb] = lane
    return table


def shards(panel_left, panel_right, amplitudes, eps_virtual, eps_occupied, pair_list, blocks):
    y, zh, x, zl, core = (lax.axis_index(name) for name in ALL)
    z = zh * 2 + zl
    panels = jnp.stack([panel_left[:, 0, :], panel_right[:, 0, :]])
    panels = jnp.pad(panels, ((0, 0), (0, 4 * QP - panels.shape[1]), (0, 0)))
    panels = jnp.transpose(panels.reshape(2, 4, QP, W), (1, 0, 3, 2))
    part = lambda k: lax.dynamic_index_in_dim(panels, (z + k) % 4, 0, keepdims=False)
    near_z = [shift(part(1), Z, 1), shift(part(3), Z, -1)]
    amps = lax.all_gather(jnp.transpose(amplitudes, (1, 0, 2)), "x", axis=0)
    opposite = gate([part(2)], near_z)[0]
    pieces = [part(0)] + near_z + [shift(opposite, Z, 2)]
    amps = lax.all_gather(amps, "y", axis=0)
    left = jnp.stack([piece[0] for piece in pieces])
    right = jnp.stack([piece[1] for piece in pieces])
    left_s, right_s = swap(left), swap(right)
    amps = lax.all_gather(gate([amps], [left_s, right_s], 58 * 2**20)[0], ("zh", "zl", "c"), axis=0)
    left_1, right_1 = onward(left, "x"), onward(right, "y")
    left_1s, right_1s = onward(left_s, "x"), onward(right_s, "y")
    right_1p = swap(right_1)
    left_2, right_2 = onward(left_1, "x"), onward(right_1, "y")
    cores = [core, 1 - core, core, 1 - core, 1 - core, core, core, 1 - core]
    zs = [(z + k) % 4 for k in RING]
    place = jnp.stack(zs + cores + [(k // 2) * 16 + (k % 2) * 4 for k in zs]).astype(jnp.int32)
    x1 = integrals(first_kernel, ROWS1, place, (left, left_1), (right, right_s, right_1))
    right_1s = gate([right_1s], [x1])[0]
    rights = (right, right_s, right_1, right_1s, right_1p, swap(right_1s))
    x2 = integrals(second_kernel, ROWS2, place, (left, left_1, left_1s), rights)
    right_2 = gate([right_2], [x2])[0]
    rights = rights + (right_2, swap(right_2))
    partial = far_ladder(place, x1, x2, (left, left_1, left_1s, left_2), amps, rights)
    gathered = lax.all_to_all(partial.reshape(32, 16, 256), ("zh", "x", "zl", "c"), 0, 0, tiled=True)
    lanes = lax.dynamic_index_in_dim(jnp.array(lane_table()), y, 0, keepdims=False)
    pick = (lanes[:, :, None, :] == jnp.arange(256, dtype=jnp.int32)[None, None, :, None]).astype(jnp.bfloat16)
    parts = jnp.einsum("hxlkpj,xkjm->hlxpm", gathered.reshape(2, 4, 2, 2, 16, 256), pick, preferred_element_type=jnp.float32)
    block = jnp.sum(parts, axis=(0, 1)).reshape(4, 16, 16, 8, 4)
    block = jnp.transpose(block, (1, 2, 3, 0, 4)).reshape(16, 16, W)
    first = lax.dynamic_slice_in_dim(eps_virtual, blocks[0] * W + (y * 2 + zh) * 16, 16)
    second = lax.dynamic_slice_in_dim(eps_virtual, blocks[1] * W, W)
    pairs = lax.dynamic_slice_in_dim(pair_list, ((x * 2 + zl) * 2 + core) * 16, 16, axis=0)
    levels = jnp.arange(eps_occupied.shape[0], dtype=jnp.int32)
    picked = jnp.where(pairs[:, :, None] == levels[None, None, :], eps_occupied[None, None, :], 0.0)
    pair_sum = jnp.sum(picked, axis=(1, 2))
    denominator = first[None, :, None] + second[None, None, :] - pair_sum[:, None, None]
    return (block / denominator).astype(jnp.bfloat16)


def solution(mesh):
    fine = Mesh(mesh.devices.reshape(4, 2, 4, 2, 2), ALL)
    return jax.shard_map(
        shards,
        mesh=fine,
        in_specs=(
            P(None, ALL, None),
            P(None, ALL, None),
            P(("x", "zl", "c"), ("y", "zh"), None),
            P(),
            P(),
            P(),
            P(),
        ),
        out_specs=P(("x", "zl", "c"), ("y", "zh"), None),
        check_vma=False,
    )
```

```python
import jax
import jax.numpy as jnp
import numpy as np
from jax import lax
from jax.experimental import pallas as pl
from jax.experimental.pallas import tpu as pltpu
from jax.sharding import Mesh, PartitionSpec as P

Z = ("zh", "zl")
ALL = ("y", "zh", "x", "zl", "c")
RING = (0, 3, 1, 2)
QP = 1280
W = 128
CC = 32
ROWS1, ROWS2, ROWS3 = 96, 192, 224
FIRST = ((0, 1, 2), (3, 4, 5), (6, 7))
ANYWHERE = pl.BlockSpec(memory_space=pl.ANY)
SCALARS = pl.BlockSpec(memory_space=pltpu.SMEM)
LIMIT = 55 * 2**20


def gate(values, after, limit=2**20):
    count = len(values)

    def nothing(*refs):
        pass

    return pl.pallas_call(
        nothing,
        out_shape=[jax.ShapeDtypeStruct(v.shape, v.dtype) for v in values],
        in_specs=[ANYWHERE] * (count + len(after)),
        out_specs=[ANYWHERE] * count,
        input_output_aliases={k: k for k in range(count)},
        compiler_params=pltpu.CompilerParams(vmem_limit_bytes=limit),
        name="gate",
    )(*values, *after)


def times(left, right):
    rows = left.shape[0] * W if left.ndim == 3 else left.shape[0] * left.shape[1] * W
    return lax.dot_general(
        left.reshape(rows, QP), right.reshape(4 * W, QP), (((1,), (1,)), ((), ())), preferred_element_type=jnp.float32
    )


def pair_integrals(place, lefts, right, scr, stride, first):
    m = times(lefts, right)
    for u in range(2):
        for za in range(4):
            for zb in range(4):
                row = first + place[12 + za] + u * 8 + place[zb]
                k = u * 4 + za
                scr[pl.ds(row, W, stride=stride), :] = m[k * W : (k + 1) * W, zb * W : (zb + 1) * W]


def single_integrals(place, left, right, core, scr, stride, first):
    m = times(left, right)
    for za in range(4):
        for zb in range(4):
            row = first + place[za] * 8 + place[zb] * 2 + core
            scr[pl.ds(row, W, stride=stride), :] = m[za * W : (za + 1) * W, zb * W : (zb + 1) * W]


def round_out(scr, xbuf, xs, rows, sems):
    quarter = W // 4
    stores = [
        pltpu.make_async_copy(xbuf.at[pl.ds(k * quarter, quarter)], xs.at[pl.ds(k * quarter, quarter)], sems.at[k]) for k in range(4)
    ]
    for k in range(4):

        def convert(c, carry):
            start = pl.multiple_of(c * (rows + 8), 8)
            xbuf[c] = scr[pl.ds(start, rows), :].astype(jnp.bfloat16)
            return carry

        lax.fori_loop(k * quarter, (k + 1) * quarter, convert, 0, unroll=16)
        stores[k].start()
    for store in stores:
        store.wait()


def first_kernel(place, l0, l1, *refs):
    rights, (xs, lbuf, rbuf, scr, xbuf, sems, out_sems) = refs[:3], refs[3:]
    copies = [pltpu.make_async_copy(ref, lbuf.at[u], sems.at[3 + u]) for u, ref in enumerate((l0, l1))]
    copies += [pltpu.make_async_copy(ref, rbuf.at[g], sems.at[g]) for g, ref in enumerate(rights)]
    for copy in copies:
        copy.start()
    for copy in copies[:2]:
        copy.wait()

    def block(g, carry):
        pltpu.make_async_copy(l0, rbuf.at[g], sems.at[g]).wait()
        pair_integrals(place, lbuf[...], rbuf[g], scr, ROWS1 + 8, g * 32)
        return carry

    lax.fori_loop(0, 3, block, 0)
    round_out(scr, xbuf, xs, ROWS1, out_sems)


def second_kernel(place, l0, l1, l2, *refs):
    rights, (xs, lbuf, rbuf, scr, xbuf, sems, out_sems) = refs[:6], refs[6:]
    copies = [pltpu.make_async_copy(ref, lbuf.at[u], sems.at[6 + u]) for u, ref in enumerate((l0, l1, l2))]
    copies += [pltpu.make_async_copy(rights[g], rbuf.at[g], sems.at[g]) for g in (3, 4, 5, 0, 1, 2)]
    for copy in copies:
        copy.start()
    for copy in copies[:6]:
        copy.wait()

    def pairs(k, carry):
        pair_integrals(place, lbuf[:2], rbuf[3 + k], scr, ROWS2 + 8, k * 32)
        return carry

    lax.fori_loop(0, 3, pairs, 0)
    for copy in copies[6:]:
        copy.wait()

    def singles(g, carry):
        single_integrals(place, lbuf[2], rbuf[g], place[4 + g], scr, ROWS2 + 8, 96 + (g // 2) * 32)
        return carry

    lax.fori_loop(0, 6, singles, 0)
    round_out(scr, xbuf, xs, ROWS2, out_sems)


def integrals(kernel, rows, place, lefts, rights):
    units, count = len(lefts), len(rights)
    return pl.pallas_call(
        kernel,
        out_shape=jax.ShapeDtypeStruct((W, rows, W), jnp.bfloat16),
        in_specs=[SCALARS] + [ANYWHERE] * (units + count),
        out_specs=pl.BlockSpec(memory_space=pltpu.HBM),
        scratch_shapes=[
            pltpu.VMEM((units, 4, W, QP), jnp.bfloat16),
            pltpu.VMEM((count, 4, W, QP), jnp.bfloat16),
            pltpu.VMEM((W * (rows + 8), W), jnp.float32),
            pltpu.VMEM((W, rows, W), jnp.bfloat16),
            pltpu.SemaphoreType.DMA((units + count,)),
            pltpu.SemaphoreType.DMA((4,)),
        ],
        compiler_params=pltpu.CompilerParams(vmem_limit_bytes=(26 if units == 2 else 34) * 2**20),
        cost_estimate=pl.CostEstimate(flops=10**6, bytes_accessed=10**4, transcendentals=0),
        name="integrals%d" % units,
    )(place, *lefts, *rights)


def far_kernel(place, x1, x2, l0, l1, l2, l3, amps, *refs):
    rights, (out, lbuf, rbuf, tbuf, xbuf1, xbuf2, scr, acc, sems) = refs[:8], refs[8:]
    copies_l = [pltpu.make_async_copy(ref, lbuf.at[u], sems.at[8 + u]) for u, ref in enumerate((l0, l1, l2, l3))]
    copies_r = [pltpu.make_async_copy(ref, rbuf.at[g], sems.at[g]) for g, ref in enumerate(rights)]
    later = [
        pltpu.make_async_copy(amps, tbuf, sems.at[12]),
        pltpu.make_async_copy(x1, xbuf1, sems.at[13]),
        pltpu.make_async_copy(x2, xbuf2, sems.at[14]),
    ]
    soon = copies_l[:2] + copies_r[6:] + copies_l[2:]
    for copy in soon + copies_r[:6] + later:
        copy.start()
    stride = ROWS3 + 8
    for copy in soon[:4]:
        copy.wait()

    def pairs(k, carry):
        pair_integrals(place, lbuf[:2], rbuf[6 + k], scr, stride, k * 32)
        return carry

    lax.fori_loop(0, 2, pairs, 0)
    for copy in soon[4:]:
        copy.wait()

    def opposite(g, carry):
        single_integrals(place, lbuf[2], rbuf[g], place[4 + g], scr, stride, 64)
        return carry

    lax.fori_loop(6, 8, opposite, 0)

    def last(g, carry):
        @pl.when(g < 6)
        def _():
            pltpu.make_async_copy(l0, rbuf.at[g], sems.at[g]).wait()

        single_integrals(place, lbuf[3], rbuf[g], place[4 + g], scr, stride, 96 + (g // 2) * 32)
        return carry

    lax.fori_loop(0, 8, last, 0)
    for copy in later:
        copy.wait()
    acc[...] = jnp.zeros_like(acc)

    def contract(step, carry):
        x = []
        t = []
        for k in range(CC):
            c = step * CC + k
            groups = []
            for values in (
                xbuf1[c],
                xbuf2[c],
                scr[pl.ds(pl.multiple_of(c * stride, 8), ROWS3), :].astype(jnp.bfloat16),
            ):
                groups += [values[g * 32 : g * 32 + 32] for g in range(values.shape[0] // 32)]
            x.append(jnp.concatenate([group[zh * 16 : zh * 16 + 16] for zh in range(2) for group in groups], axis=0))
            y, zh, low = c // 32, (c // 16) % 2, c % 16
            t.append(
                jnp.concatenate(
                    [tbuf[(zh * 2 + zl) * 2 + core, y, xx, low] for xx in range(4) for zl in range(2) for core in range(2)],
                    axis=0,
                )
            )
        acc[...] += lax.dot_general(
            jnp.concatenate(t, axis=1),
            jnp.concatenate(x, axis=1),
            (((1,), (1,)), ((), ())),
            preferred_element_type=jnp.float32,
        )
        return carry

    lax.fori_loop(0, W // CC, contract, 0)
    for zh in range(2):
        out[zh] = acc[:, zh * 256 : (zh + 1) * 256].astype(out.dtype).reshape(16, 16, 256)


def far_ladder(place, x1, x2, lefts, amps, rights):
    return pl.pallas_call(
        far_kernel,
        out_shape=jax.ShapeDtypeStruct((2, 16, 16, 256), jnp.bfloat16),
        in_specs=[SCALARS] + [ANYWHERE] * 15,
        out_specs=pl.BlockSpec(memory_space=pltpu.VMEM),
        scratch_shapes=[
            pltpu.VMEM((4, 4, W, QP), jnp.bfloat16),
            pltpu.VMEM((8, 4, W, QP), jnp.bfloat16),
            pltpu.VMEM((8, 4, 4, 16, 16, W), jnp.bfloat16),
            pltpu.VMEM((W, ROWS1, W), jnp.bfloat16),
            pltpu.VMEM((W, ROWS2, W), jnp.bfloat16),
            pltpu.VMEM((W * (ROWS3 + 8), W), jnp.float32),
            pltpu.VMEM((256, 512), jnp.float32),
            pltpu.SemaphoreType.DMA((15,)),
        ],
        compiler_params=pltpu.CompilerParams(vmem_limit_bytes=LIMIT),
        cost_estimate=pl.CostEstimate(flops=15 * 10**9, bytes_accessed=10**7, transcendentals=0),
        name="far_ladder",
    )(place, x1, x2, *lefts, amps, *rights)


def swap(value):
    return lax.ppermute(value, "c", [(0, 1), (1, 0)])


def shift(value, axis, step):
    return lax.ppermute(value, axis, [(i, (i + step) % 4) for i in range(4)])


def onward(value, axis):
    pairs = [(i * 2 + c, (i + 1 - 2 * c) % 4 * 2 + c) for i in range(4) for c in range(2)]
    return lax.ppermute(value, (axis, "c"), pairs)


def lane_table():
    table = np.full((4, 4, 2, 512), -1, np.int32)
    group_of = {block: k for k, block in enumerate(FIRST[0])}
    group_of.update({FIRST[1][k]: 3 + k for k in range(3)})
    group_of.update({FIRST[2][k]: 9 + k for k in range(2)})
    for y, x, far, zl, c, yb, zb, cb in np.ndindex(4, 4, 4, 2, 2, 4, 4, 2):
        step = (far - x) % 4
        if step in (0, 2):
            core, unit = c, (0 if step == 0 else 3)
        else:
            core = 0 if step == 3 else 1
            unit = 1 if core == c else 2
        slot = ({0: 0, 3: 1, 1: 2, 2: 3} if core == 0 else {0: 0, 1: 1, 3: 2, 2: 3})[(yb - y) % 4]
        own = (cb == core) != (slot == 2)
        if unit < 2:
            lane = group_of[slot * 2 + (0 if own else 1)] * 16 + unit * 8 + zl * 4 + zb
        else:
            group = (6, 7, 8, 11)[slot] if unit == 2 else 12 + slot
            lane = group * 16 + zl * 8 + zb * 2 + cb
        table[y, x, core, ((far * 2 + zl) * 2 + c) * 32 + (yb * 4 + zb) * 2 + cb] = lane
    return table


def shards(panel_left, panel_right, amplitudes, eps_virtual, eps_occupied, pair_list, blocks):
    y, zh, x, zl, core = (lax.axis_index(name) for name in ALL)
    z = zh * 2 + zl
    panels = jnp.stack([panel_left[:, 0, :], panel_right[:, 0, :]])
    panels = jnp.pad(panels, ((0, 0), (0, 4 * QP - panels.shape[1]), (0, 0)))
    panels = jnp.transpose(panels.reshape(2, 4, QP, W), (1, 0, 3, 2))
    part = lambda k: lax.dynamic_index_in_dim(panels, (z + k) % 4, 0, keepdims=False)
    near_z = [shift(part(1), Z, 1), shift(part(3), Z, -1)]
    amps = lax.all_gather(jnp.transpose(amplitudes, (1, 0, 2)), "x", axis=0)
    opposite = gate([part(2)], near_z)[0]
    pieces = [part(0)] + near_z + [shift(opposite, Z, 2)]
    amps = lax.all_gather(amps, "y", axis=0)
    left = jnp.stack([piece[0] for piece in pieces])
    right = jnp.stack([piece[1] for piece in pieces])
    left_s, right_s = swap(left), swap(right)
    amps = lax.all_gather(gate([amps], [left_s, right_s], 58 * 2**20)[0], ("zh", "zl", "c"), axis=0)
    left_1, right_1 = onward(left, "x"), onward(right, "y")
    left_1s, right_1s = onward(left_s, "x"), onward(right_s, "y")
    right_1p = swap(right_1)
    left_2, right_2 = onward(left_1, "x"), onward(right_1, "y")
    cores = [core, 1 - core, core, 1 - core, 1 - core, core, core, 1 - core]
    zs = [(z + k) % 4 for k in RING]
    place = jnp.stack(zs + cores + [(k // 2) * 16 + (k % 2) * 4 for k in zs]).astype(jnp.int32)
    x1 = integrals(first_kernel, ROWS1, place, (left, left_1), (right, right_s, right_1))
    right_1s = gate([right_1s], [x1])[0]
    rights = (right, right_s, right_1, right_1s, right_1p, swap(right_1s))
    x2 = integrals(second_kernel, ROWS2, place, (left, left_1, left_1s), rights)
    right_2 = gate([right_2], [x2])[0]
    rights = rights + (right_2, swap(right_2))
    partial = far_ladder(place, x1, x2, (left, left_1, left_1s, left_2), amps, rights)
    gathered = lax.all_to_all(partial.reshape(32, 16, 256), ("zh", "x", "zl", "c"), 0, 0, tiled=True)
    lanes = lax.dynamic_index_in_dim(jnp.array(lane_table()), y, 0, keepdims=False)
    pick = (lanes[:, :, None, :] == jnp.arange(256, dtype=jnp.int32)[None, None, :, None]).astype(jnp.bfloat16)
    parts = jnp.einsum("hxlkpj,xkjm->hlxpm", gathered.reshape(2, 4, 2, 2, 16, 256), pick, preferred_element_type=jnp.float32)
    block = jnp.sum(parts, axis=(0, 1)).reshape(4, 16, 16, 8, 4)
    block = jnp.transpose(block, (1, 2, 3, 0, 4)).reshape(16, 16, W)
    first = lax.dynamic_slice_in_dim(eps_virtual, blocks[0] * W + (y * 2 + zh) * 16, 16)
    second = lax.dynamic_slice_in_dim(eps_virtual, blocks[1] * W, W)
    pairs = lax.dynamic_slice_in_dim(pair_list, ((x * 2 + zl) * 2 + core) * 16, 16, axis=0)
    levels = jnp.arange(eps_occupied.shape[0], dtype=jnp.int32)
    picked = jnp.where(pairs[:, :, None] == levels[None, None, :], eps_occupied[None, None, :], 0.0)
    pair_sum = jnp.sum(picked, axis=(1, 2))
    denominator = first[None, :, None] + second[None, None, :] - pair_sum[:, None, None]
    return (block / denominator).astype(jnp.bfloat16)


def solution(mesh):
    fine = Mesh(mesh.devices.reshape(4, 2, 4, 2, 2), ALL)
    return jax.shard_map(
        shards,
        mesh=fine,
        in_specs=(
            P(None, ALL, None),
            P(None, ALL, None),
            P(("x", "zl", "c"), ("y", "zh"), None),
            P(),
            P(),
            P(),
            P(),
        ),
        out_specs=P(("x", "zl", "c"), ("y", "zh"), None),
        check_vma=False,
    )
```
